512 devices in a mesh: ctx: 64 (over y, z), head: 8 (over x, core).
Axes of the slice: x: 4, y: 4, z: 16, core: 2. Of those that a mesh axis runs over, the one named last changes fastest.
Arguments:
- queries: bfloat16 [32768, 64, 128], P('ctx', 'head'), may hold values from -120 to 120
- key_rows: bfloat16 [32768, 64, 128], P('ctx', 'head'), may hold values from -6 to 6
- value_rows: bfloat16 [32768, 64, 128], P('ctx', 'head'), may hold values from -6 to 6
- selection: int32 [64, 64, 3], P(None, 'head'), may hold values from 0 to 62, as said below
Outputs:
- attended: bfloat16 [32768, 64, 128], P('ctx', 'head')
- affinity: bfloat16 [32768, 64, 64], P('ctx', 'head')
The draws below stay inside these ranges and needn't reach their ends.
Inputs may be any that keep to these rules, and one draw needn't show every extreme that they name: `selection`: for each query block and head the 3 entries are distinct; every block's list after the first holds the block just before it; entries at or after the query's own block occur only in the first 3 blocks.
All inputs are finite; a program needn't handle non-finite values.
Results may differ from the reference program's by a relative error of at most 0.011.
Values may be sent and summed in bfloat16 or wider, within the bound.
No kernel may reach another device: no remote copies, remote signals or barrier semaphores. Data moves between devices by JAX's collectives and lax.ppermute only.
A program may use at most 64 MiB of HBM per device.

```python
import jax
import jax.numpy as jnp
from jax import lax

HD = 128
BLOCK = 512
TOPK = 3
HEADS = 64
NB = 64
TOKENS = 32768


def base_fields(key):
    first_key = jax.random.fold_in(key, 11)
    second_key = jax.random.fold_in(key, 12)
    query_field = jax.random.truncated_normal(first_key, -6.0, 6.0, (TOKENS, HEADS, HD), jnp.float32)
    key_field = jax.random.truncated_normal(second_key, -6.0, 6.0, (TOKENS, HEADS, HD), jnp.float32)
    return (query_field, key_field)


def draw_queries(key, part):
    query_field, key_field = base_fields(key)
    return query_field.astype(jnp.bfloat16)


def draw_key_rows(key, part):
    query_field, key_field = base_fields(key)
    return key_field.astype(jnp.bfloat16)


def draw_selection(key, part):
    key = jax.random.fold_in(key, 33)
    pick_key, score_key = jax.random.split(key)
    popular = (jax.random.randint(pick_key, (NB,), 0, 6) == 0).astype(jnp.int32)
    raw_scores = jax.random.randint(score_key, (NB, HEADS, NB), 0, 4096)
    raw_scores = raw_scores // (1 + 7 * popular)[None, None, :]
    block_ids = jnp.arange(NB, dtype=jnp.int32)[:, None, None]
    candidate = jnp.arange(NB, dtype=jnp.int32)[None, None, :]
    ceiling = jnp.maximum(block_ids, TOPK)
    ranked = raw_scores * NB + candidate
    ranked = jnp.where(candidate >= ceiling, 4096 * NB + NB + candidate, ranked)
    ranked = jnp.where(candidate == block_ids - 1, -1, ranked)
    ordered = jnp.argsort(ranked, axis=-1)[..., :TOPK]
    return ordered.astype(jnp.int32)


def steps_of(rng, dims, cuts, smallest, largest):
    loudness = 1.0
    for dim, parts in cuts:
        steps = jax.random.uniform(jax.random.fold_in(jax.random.fold_in(rng, 6), dim), (parts,), jnp.float32, smallest / len(cuts), largest / len(cuts))
        loudness = loudness * jnp.repeat(jnp.exp(steps), dims[dim] // parts).reshape((-1,) + (1,) * (len(dims) - 1 - dim))
    return loudness


def noise(stream_key, dims, deviation, most, pieces=(), kind=jnp.bfloat16):
    values = jax.random.normal(stream_key, dims, jnp.float32) * deviation
    if len(pieces) > 0:
        values = steps_of(stream_key, dims, pieces, -0.22, 0.18) * values
    return jnp.clip(values, min=-most, max=most).astype(kind)


def setup_inputs(seed: int = 0) -> dict:
    key_of = jax.random.split(jax.random.key(seed), 5)
    queries = draw_queries(jax.random.fold_in(key_of[4], 71), 0)
    key_rows = draw_key_rows(jax.random.fold_in(key_of[4], 71), 0)
    value_rows = noise(key_of[2], (TOKENS, HEADS, HD), 1.0, 6.0, ((0, 64), (1, 8)))
    selection = draw_selection(jax.random.fold_in(key_of[4], 71), 0)
    return {"queries": queries, "key_rows": key_rows, "value_rows": value_rows, "selection": selection}


def attend(query_block, key_block, value_block, usable):
    slots, block_len, head_dim = key_block.shape
    flat_keys = key_block.reshape(slots * block_len, head_dim)
    flat_values = value_block.reshape(slots * block_len, head_dim)
    scores = lax.dot_general(query_block, flat_keys, (((1,), (1,)), ((), ())), preferred_element_type=jnp.float32)
    scores = scores * (head_dim ** -0.5)
    row_ids = jnp.arange(block_len)[:, None]
    col_ids = jnp.arange(slots * block_len)[None, :]
    slot_index = col_ids // block_len
    offset = col_ids % block_len
    allowed = jnp.where(slot_index == 0, offset <= row_ids, usable[slot_index])
    scores = jnp.where(allowed, scores, -jnp.inf)
    row_max = jnp.max(scores, axis=-1, keepdims=True)
    weights = jnp.exp(scores - row_max)
    denominator = jnp.sum(weights, axis=-1, keepdims=True)
    weighted = jnp.dot(weights.astype(jnp.bfloat16), flat_values, preferred_element_type=jnp.float32)
    return (weighted / denominator).astype(jnp.bfloat16)


def reference(queries, key_rows, value_rows, selection):
    key_blocks = key_rows.reshape(NB, BLOCK, HEADS, HD)
    pooled = (jnp.sum(key_blocks, axis=1, dtype=jnp.float32) / BLOCK).astype(jnp.bfloat16)
    affinity = jnp.einsum("thd,bhd->thb", queries.astype(jnp.float32), pooled.astype(jnp.float32), precision=lax.Precision.HIGHEST)
    token_block = jnp.arange(TOKENS) // BLOCK
    causal = jnp.arange(NB)[None, None, :] <= token_block[:, None, None]
    affinity = jnp.where(causal, affinity, jnp.zeros_like(affinity)).astype(jnp.bfloat16)
    keys_by_head = key_blocks.transpose(2, 0, 1, 3)
    values_by_head = value_rows.reshape(NB, BLOCK, HEADS, HD).transpose(2, 0, 1, 3)
    queries_by_block = queries.reshape(NB, BLOCK, HEADS, HD).transpose(0, 2, 1, 3)
    head_ids = jnp.arange(HEADS, dtype=jnp.int32)

    def one_block(block_id):
        chosen = selection[block_id]
        slot_table = jnp.concatenate([jnp.full((HEADS, 1), block_id, jnp.int32), chosen], axis=1)
        chosen_keys = keys_by_head[head_ids[:, None], slot_table]
        chosen_values = values_by_head[head_ids[:, None], slot_table]
        usable = jnp.concatenate([jnp.ones((HEADS, 1), bool), chosen < block_id], axis=1)
        return jax.vmap(attend)(queries_by_block[block_id], chosen_keys, chosen_values, usable)

    outputs = lax.map(one_block, jnp.arange(NB, dtype=jnp.int32))
    attended = outputs.transpose(0, 2, 1, 3).reshape(TOKENS, HEADS, HD)
    return attended, affinity
```

```python
import functools

import jax
import jax.numpy as jnp
from jax import lax
from jax.experimental import pallas as pl
from jax.experimental.pallas import tpu as pltpu
from jax.sharding import PartitionSpec as P

LOG2E = 1.4426950408889634
MASKED = -1e30


def pick_kernel(blocks, table_ref, parts_ref, out_ref):
    head = pl.program_id(0)

    def one(c, carry):
        base = (head * blocks + c) * 2
        first = parts_ref[table_ref[base], 0].astype(jnp.float32)
        second = parts_ref[table_ref[base + 1], 0].astype(jnp.float32)
        half = first.shape[0] // 2
        out_ref[c, 0, 0] = jnp.concatenate([first[:half], second[:half]], 0).astype(jnp.bfloat16)
        out_ref[c, 0, 1] = jnp.concatenate([first[half:], second[half:]], 0).astype(jnp.bfloat16)
        return carry

    lax.fori_loop(0, blocks, one, 0, unroll=8)


def near_kernel(scale, flag_ref, q_ref, k_ref, v_ref, pk_ref, pv_ref, acc_ref, stat_ref):
    q = q_ref[0]
    rows = q.shape[0]
    dims = (((1,), (1,)), ((), ()))
    own = lax.dot_general(q, k_ref[0], dims, preferred_element_type=jnp.float32)
    row_ids = lax.broadcasted_iota(jnp.int32, own.shape, 0)
    col_ids = lax.broadcasted_iota(jnp.int32, own.shape, 1)
    own = jnp.where(col_ids <= row_ids, own, MASKED)
    before = lax.dot_general(q, pk_ref[0], dims, preferred_element_type=jnp.float32)
    before = jnp.where(flag_ref[0] > 0, before, MASKED)
    top = jnp.maximum(jnp.max(own, 1, keepdims=True), jnp.max(before, 1, keepdims=True))
    own = jnp.exp2((own - top) * scale)
    before = jnp.exp2((before - top) * scale)
    total = jnp.sum(own, 1, keepdims=True) + jnp.sum(before, 1, keepdims=True)
    acc = jnp.dot(own.astype(jnp.bfloat16), v_ref[0], preferred_element_type=jnp.float32)
    acc += jnp.dot(before.astype(jnp.bfloat16), pv_ref[0], preferred_element_type=jnp.float32)
    acc_ref[0] = acc
    lane = lax.broadcasted_iota(jnp.int32, (rows, stat_ref.shape[2]), 1)
    stat_ref[0] = jnp.where(lane < stat_ref.shape[2] // 2, top, total)


def far_kernel(scale, flag_ref, q_ref, kv_ref, acc_ref, stat_ref, out_ref):
    head = pl.program_id(0)
    q = q_ref[0]
    keys = kv_ref[:, 0, 0]
    values = kv_ref[:, 0, 1]
    pair, head_dim = keys.shape[1:]
    keys = keys.reshape(-1, head_dim)
    values = values.reshape(-1, head_dim)
    scores = lax.dot_general(
        q, keys, (((1,), (1,)), ((), ())), preferred_element_type=jnp.float32
    )
    col = lax.broadcasted_iota(jnp.int32, (1, keys.shape[0]), 1) % pair
    allowed = jnp.where(col < pair // 2, flag_ref[2 * head], flag_ref[2 * head + 1])
    scores = jnp.where(allowed > 0, scores, MASKED)
    half = stat_ref.shape[2] // 2
    top_before = stat_ref[0][:, :1]
    total_before = stat_ref[0][:, half : half + 1]
    top = jnp.maximum(jnp.max(scores, 1, keepdims=True), top_before)
    weights = jnp.exp2((scores - top) * scale)
    shrink = jnp.exp2((top_before - top) * scale)
    total = total_before * shrink + jnp.sum(weights, 1, keepdims=True)
    acc = jnp.dot(weights.astype(jnp.bfloat16), values, preferred_element_type=jnp.float32)
    acc += acc_ref[0] * shrink
    out_ref[0] = (acc / total).astype(jnp.bfloat16)


def body(queries, key_rows, value_rows, selection):
    ctx_size = lax.axis_size("ctx")
    block_len, heads, head_dim = queries.shape
    blocks, _, topk = selection.shape
    assert blocks == ctx_size and topk == 3
    slice_rows = block_len // ctx_size
    position = lax.axis_index("ctx")
    scale = LOG2E * head_dim**-0.5
    bf16 = jnp.bfloat16
    vmem = pltpu.CompilerParams(vmem_limit_bytes=48 * 1024 * 1024)

    def slices(x):
        return x.reshape(ctx_size, slice_rows, heads, head_dim).transpose(0, 2, 1, 3)

    send = jnp.concatenate([slices(key_rows), slices(value_rows)], axis=2)
    parts = lax.all_to_all(send, "ctx", split_axis=0, concat_axis=0, tiled=True)

    keys = key_rows.transpose(1, 0, 2)
    values = value_rows.transpose(1, 0, 2)
    steps = [(i, i + 1) for i in range(ctx_size - 1)]
    prev_keys = lax.ppermute(keys, "ctx", steps)
    prev_values = lax.ppermute(values, "ctx", steps)

    pooled = (jnp.sum(key_rows, axis=0, dtype=jnp.float32) / block_len).astype(bf16)
    pooled_all = lax.all_gather(pooled[None], "ctx", axis=0, tiled=True)

    owner = jnp.arange(blocks, dtype=jnp.int32)[:, None]
    first = jnp.where(selection[:, :, 0] == owner - 1, selection[:, :, 1], selection[:, :, 0])
    last = jnp.where(selection[:, :, 2] == owner - 1, selection[:, :, 1], selection[:, :, 2])
    picks = jnp.stack([first, last], axis=2)
    table = picks.transpose(1, 0, 2).reshape(-1)
    mine = lax.dynamic_index_in_dim(picks, position, 0, keepdims=False)
    far_flags = (mine < position).astype(jnp.int32).reshape(-1)
    near_flag = (position > 0).astype(jnp.int32).reshape(1)

    picked = pl.pallas_call(
        functools.partial(pick_kernel, blocks),
        grid_spec=pltpu.PrefetchScalarGridSpec(
            num_scalar_prefetch=1,
            grid=(heads,),
            in_specs=[
                pl.BlockSpec((blocks, 1, 2 * slice_rows, head_dim), lambda h, t: (0, h, 0, 0))
            ],
            out_specs=pl.BlockSpec(
                (blocks, 1, 2, 2 * slice_rows, head_dim), lambda h, t: (0, h, 0, 0, 0)
            ),
        ),
        out_shape=jax.ShapeDtypeStruct((blocks, heads, 2, 2 * slice_rows, head_dim), bf16),
        compiler_params=vmem,
        name="pick",
    )(table, parts)
    fetched = lax.all_to_all(picked, "ctx", split_axis=0, concat_axis=0, tiled=True)

    q = queries.transpose(1, 0, 2)
    per_head = jnp.einsum("htd,bhd->htb", q, pooled_all, preferred_element_type=jnp.float32)
    causal = jnp.arange(blocks, dtype=jnp.int32) <= position
    affinity = jnp.where(causal, per_head, 0.0).astype(bf16).transpose(1, 0, 2)

    whole = pl.BlockSpec((1, block_len, head_dim), lambda h, t: (h, 0, 0))
    acc, stat = pl.pallas_call(
        functools.partial(near_kernel, scale),
        grid_spec=pltpu.PrefetchScalarGridSpec(
            num_scalar_prefetch=1, grid=(heads,), in_specs=[whole] * 5, out_specs=[whole, whole]
        ),
        out_shape=[jax.ShapeDtypeStruct((heads, block_len, head_dim), jnp.float32)] * 2,
        compiler_params=vmem,
        cost_estimate=pl.CostEstimate(
            flops=heads * block_len * block_len * head_dim * 8,
            bytes_accessed=heads * block_len * head_dim * 18,
            transcendentals=heads * block_len * block_len * 2,
        ),
        name="near",
    )(near_flag, q, keys, values, prev_keys, prev_values)
    out = pl.pallas_call(
        functools.partial(far_kernel, scale),
        grid_spec=pltpu.PrefetchScalarGridSpec(
            num_scalar_prefetch=1,
            grid=(heads,),
            in_specs=[
                whole,
                pl.BlockSpec(
                    (ctx_size, 1, 2, 2 * slice_rows, head_dim), lambda h, t: (0, h, 0, 0, 0)
                ),
                whole,
                whole,
            ],
            out_specs=whole,
        ),
        out_shape=jax.ShapeDtypeStruct((heads, block_len, head_dim), bf16),
        compiler_params=vmem,
        cost_estimate=pl.CostEstimate(
            flops=heads * block_len * block_len * head_dim * 8,
            bytes_accessed=heads * block_len * head_dim * 18,
            transcendentals=heads * block_len * block_len * 2,
        ),
        name="far",
    )(far_flags, q, fetched, acc, stat)
    return out.transpose(1, 0, 2), affinity


def solution(mesh):
    in_specs = (
        P("ctx", "head", None),
        P("ctx", "head", None),
        P("ctx", "head", None),
        P(None, "head", None),
    )
    out_specs = (P("ctx", "head", None), P("ctx", "head", None))
    return jax.shard_map(body, mesh=mesh, in_specs=in_specs, out_specs=out_specs, check_vma=False)
```

```python
import functools

import jax
import jax.numpy as jnp
from jax import lax
from jax.experimental import pallas as pl
from jax.experimental.pallas import tpu as pltpu
from jax.sharding import PartitionSpec as P

LOG2E = 1.4426950408889634
MASKED = -1e30
ROWS = 16
ACROSS = (((1,), (1,)), ((), ()))
F32 = jnp.float32
BF16 = jnp.bfloat16


def pack_kernel(k_ref, v_ref, out_ref, kt_ref, vt_ref):
    block_len, heads, head_dim = k_ref.shape
    half = block_len // ROWS

    def one(p, total):
        here = pl.ds(p * ROWS, ROWS)
        keys = k_ref[here].astype(F32)
        by_head = jnp.transpose(keys, (1, 0, 2)).astype(BF16)
        kt_ref[:, here] = by_head
        out_ref[p, : heads * ROWS] = by_head.reshape(heads * ROWS, head_dim)
        by_head = jnp.transpose(v_ref[here].astype(F32), (1, 0, 2)).astype(BF16)
        vt_ref[:, here] = by_head
        out_ref[p + half, : heads * ROWS] = by_head.reshape(heads * ROWS, head_dim)
        return total + jnp.sum(keys, 0)

    total = lax.fori_loop(0, half, one, jnp.zeros((heads, head_dim), F32), unroll=4)
    pooled = (total / block_len).astype(BF16)

    def spread(p, carry):
        out_ref[p, heads * ROWS :] = pooled
        return carry

    lax.fori_loop(0, 2 * half, spread, 0, unroll=8)


def pick_kernel(table_ref, parts_ref, out_ref):
    blocks = parts_ref.shape[0]
    base = pl.program_id(0) * blocks * 2

    def one(c, carry):
        out_ref[c, :ROWS] = parts_ref[table_ref[base + 2 * c]]
        out_ref[c, ROWS:] = parts_ref[table_ref[base + 2 * c + 1]]
        return carry

    lax.fori_loop(0, blocks, one, 0, unroll=16)


def halves(x):
    count, rows, head_dim = x.shape
    keys = x[: count // 2].reshape(count // 2 * rows, head_dim)
    values = x[count // 2 :].reshape(count // 2 * rows, head_dim)
    return keys, values


def own_kernel(scale, q_ref, kv_ref, acc_ref, stat_ref):
    keys, values = halves(kv_ref[...])
    scores = lax.dot_general(q_ref[0], keys, ACROSS, preferred_element_type=F32)
    row_ids = lax.broadcasted_iota(jnp.int32, scores.shape, 0)
    col_ids = lax.broadcasted_iota(jnp.int32, scores.shape, 1)
    scores = jnp.where(col_ids <= row_ids, scores, MASKED)
    top = jnp.max(scores, 1, keepdims=True) * scale
    weights = jnp.exp2(scores * scale - top)
    total = jnp.sum(weights, 1, keepdims=True)
    acc_ref[0] = jnp.dot(weights.astype(BF16), values, preferred_element_type=F32)
    lane = lax.broadcasted_iota(jnp.int32, stat_ref.shape[1:], 1)
    stat_ref[0] = jnp.where(lane < stat_ref.shape[2] // 2, top, total)


def before_kernel(scale, flag_ref, q_ref, k_ref, v_ref, acc_ref, stat_ref, acc_out, stat_out):
    scores = lax.dot_general(q_ref[0], k_ref[0], ACROSS, preferred_element_type=F32)
    scores = jnp.where(flag_ref[0] > 0, scores, MASKED)
    half = stat_ref.shape[2] // 2
    top_before = stat_ref[0][:, :1]
    top = jnp.maximum(jnp.max(scores, 1, keepdims=True) * scale, top_before)
    weights = jnp.exp2(scores * scale - top)
    shrink = jnp.exp2(top_before - top)
    total = jnp.sum(weights, 1, keepdims=True) + stat_ref[0][:, half : half + 1] * shrink
    acc = jnp.dot(weights.astype(BF16), v_ref[0], preferred_element_type=F32)
    acc_out[0] = acc + acc_ref[0] * shrink
    lane = lax.broadcasted_iota(jnp.int32, stat_ref.shape[1:], 1)
    stat_out[0] = jnp.where(lane < half, top, total)


def far_kernel(scale, flag_ref, q_ref, kv_ref, acc_ref, stat_ref, out_ref):
    group, block_len, head_dim = q_ref.shape
    half = stat_ref.shape[2] // 2
    first_head = pl.program_id(0) * group
    step = block_len // 2
    heads = []
    for h in range(group):
        both = [halves(kv_ref[:, (2 * h + s) * ROWS : (2 * h + s + 1) * ROWS]) for s in range(2)]
        keys = jnp.concatenate([both[0][0], both[1][0]], 0)
        values = jnp.concatenate([both[0][1], both[1][1]], 0)
        values = jnp.concatenate([values, jnp.ones_like(values)], 1)
        off = [
            jnp.where(flag_ref[2 * (first_head + h) + s] > 0, 0.0, MASKED) for s in range(2)
        ]
        col = lax.broadcasted_iota(jnp.int32, (1, keys.shape[0]), 1)
        heads.append((keys, values, jnp.where(col < block_len, off[0], off[1])))

    def score(h, start):
        keys, _, off = heads[h]
        q = q_ref[h, start : start + step]
        return lax.dot_general(q, keys, ACROSS, preferred_element_type=F32) + off

    def finish(h, start, scores):
        _, values, _ = heads[h]
        here = pl.ds(start, step)
        stat = stat_ref[h, here]
        top_before = stat[:, :1]
        top = jnp.maximum(jnp.max(scores, 1, keepdims=True) * scale, top_before)
        weights = jnp.exp2(scores * scale - top).astype(BF16)
        shrink = jnp.exp2(top_before - top)
        both = jnp.dot(weights, values, preferred_element_type=F32)
        acc = acc_ref[h, here] * shrink + both[:, :head_dim]
        total = stat[:, half : half + 1] * shrink + both[:, head_dim:]
        out_ref[h, here] = (acc / total).astype(BF16)

    todo = [(h, start) for h in range(group) for start in range(0, block_len, step)]
    scores = score(*todo[0])
    for index, item in enumerate(todo):
        following = score(*todo[index + 1]) if index + 1 < len(todo) else None
        finish(*item, scores)
        scores = following


def body(queries, key_rows, value_rows, selection):
    ctx_size = lax.axis_size("ctx")
    block_len, heads, head_dim = queries.shape
    blocks, _, topk = selection.shape
    assert blocks == ctx_size and topk == 3 and block_len == ROWS * ctx_size // 2
    position = lax.axis_index("ctx")
    scale = LOG2E * head_dim**-0.5
    params = pltpu.CompilerParams(vmem_limit_bytes=58 * 1024 * 1024)
    small = pltpu.CompilerParams(vmem_limit_bytes=32 * 1024 * 1024)

    def cost(matmuls, moved):
        return pl.CostEstimate(
            flops=heads * block_len * block_len * head_dim * 2 * matmuls,
            bytes_accessed=heads * block_len * head_dim * moved,
            transcendentals=heads * block_len * block_len * matmuls // 2,
        )

    whole = pl.BlockSpec((1, block_len, head_dim), lambda h, *_: (h, 0, 0))
    piece = pl.BlockSpec((ctx_size, ROWS, head_dim), lambda h, *_: (0, h, 0))
    pair = pl.BlockSpec((ctx_size, 2 * ROWS, head_dim), lambda h, *_: (0, h, 0))
    by_head = functools.partial(jax.ShapeDtypeStruct, (heads, block_len, head_dim))

    send, keys, values = pl.pallas_call(
        pack_kernel,
        out_shape=[
            jax.ShapeDtypeStruct((ctx_size, heads * (ROWS + 1), head_dim), BF16),
            by_head(BF16),
            by_head(BF16),
        ],
        compiler_params=params,
        name="pack",
    )(key_rows, value_rows)
    ahead = [(i, i + 1) for i in range(ctx_size - 1)]
    keys_before = lax.ppermute(keys, "ctx", ahead)
    parts = lax.all_to_all(send, "ctx", split_axis=0, concat_axis=0, tiled=True)

    owner = jnp.arange(blocks, dtype=jnp.int32)[:, None]
    first = jnp.where(selection[:, :, 0] == owner - 1, selection[:, :, 1], selection[:, :, 0])
    last = jnp.where(selection[:, :, 2] == owner - 1, selection[:, :, 1], selection[:, :, 2])
    picks = jnp.stack([first, last], axis=2)
    table = picks.transpose(1, 0, 2).reshape(-1)
    mine = lax.dynamic_index_in_dim(picks, position, 0, keepdims=False)
    usable = (mine < position).astype(jnp.int32).reshape(-1)

    q = queries.transpose(1, 0, 2)
    own_q, keys_before = lax.optimization_barrier((q, keys_before))
    own = pl.pallas_call(
        functools.partial(own_kernel, scale),
        grid=(heads,),
        in_specs=[whole, piece],
        out_specs=[whole, whole],
        out_shape=[by_head(F32), by_head(F32)],
        compiler_params=params,
        cost_estimate=cost(200, 200),
        name="own",
    )(own_q, send)
    own, values = lax.optimization_barrier((own, values))
    own, parts = lax.optimization_barrier((own, parts))
    values_before = lax.ppermute(values, "ctx", ahead)

    picked = pl.pallas_call(
        pick_kernel,
        grid_spec=pltpu.PrefetchScalarGridSpec(
            num_scalar_prefetch=1, grid=(heads,), in_specs=[piece], out_specs=pair
        ),
        out_shape=jax.ShapeDtypeStruct((blocks, heads * 2 * ROWS, head_dim), BF16),
        compiler_params=small,
        name="pick",
    )(table, parts)
    fetched = lax.all_to_all(picked, "ctx", split_axis=0, concat_axis=0, tiled=True)

    pooled = parts[:, heads * ROWS :]
    per_head = jnp.einsum("htd,bhd->htb", q, pooled, preferred_element_type=F32)
    causal = jnp.arange(blocks, dtype=jnp.int32) <= position
    affinity = jnp.where(causal, per_head, 0.0).astype(BF16).transpose(1, 0, 2)

    acc, stat = pl.pallas_call(
        functools.partial(before_kernel, scale),
        grid_spec=pltpu.PrefetchScalarGridSpec(
            num_scalar_prefetch=1, grid=(heads,), in_specs=[whole] * 5, out_specs=[whole, whole]
        ),
        out_shape=[by_head(F32), by_head(F32)],
        compiler_params=params,
        cost_estimate=cost(800, 800),
        name="before",
    )(
        (position > 0).astype(jnp.int32).reshape(1),
        q,
        keys_before,
        values_before,
        *own,
    )
    group = 2
    some = pl.BlockSpec((group, block_len, head_dim), lambda h, *_: (h, 0, 0))
    out = pl.pallas_call(
        functools.partial(far_kernel, scale),
        grid_spec=pltpu.PrefetchScalarGridSpec(
            num_scalar_prefetch=1,
            grid=(heads // group,),
            in_specs=[
                some,
                pl.BlockSpec((ctx_size, group * 2 * ROWS, head_dim), lambda h, *_: (0, h, 0)),
                some,
                some,
            ],
            out_specs=some,
        ),
        out_shape=by_head(BF16),
        compiler_params=params,
        cost_estimate=cost(4, 20),
        name="far",
    )(usable, q, fetched, acc, stat)
    return out.transpose(1, 0, 2), affinity


def solution(mesh):
    in_specs = (
        P("ctx", "head", None),
        P("ctx", "head", None),
        P("ctx", "head", None),
        P(None, "head", None),
    )
    out_specs = (P("ctx", "head", None), P("ctx", "head", None))
    return jax.shard_map(body, mesh=mesh, in_specs=in_specs, out_specs=out_specs, check_vma=False)
```

```python
import functools

import jax
import jax.numpy as jnp
from jax import lax
from jax.experimental import pallas as pl
from jax.experimental.pallas import tpu as pltpu
from jax.sharding import PartitionSpec as P

LOG2E = 1.4426950408889634
MASKED = -1e30
ROWS = 16
ACROSS = (((1,), (1,)), ((), ()))
F32 = jnp.float32
BF16 = jnp.bfloat16


def pack_kernel(q_ref, k_ref, v_ref, out_ref, qt_ref, back_ref, ahead_ref):
    block_len, heads, head_dim = k_ref.shape
    half = block_len // ROWS
    given = back_ref.shape[0]

    def one(p, total):
        here = pl.ds(p * ROWS, ROWS)
        by_head = jnp.transpose(q_ref[here].astype(F32), (1, 0, 2)).astype(BF16)
        qt_ref[:, here] = by_head
        back_ref[:, here] = by_head[:given]
        keys = k_ref[here].astype(F32)
        by_head = jnp.transpose(keys, (1, 0, 2)).astype(BF16)
        ahead_ref[0, :, here] = by_head[given:]
        out_ref[p, : heads * ROWS] = by_head.reshape(heads * ROWS, head_dim)
        by_head = jnp.transpose(v_ref[here].astype(F32), (1, 0, 2)).astype(BF16)
        ahead_ref[1, :, here] = by_head[given:]
        out_ref[p + half, : heads * ROWS] = by_head.reshape(heads * ROWS, head_dim)
        return total + jnp.sum(keys, 0)

    total = lax.fori_loop(0, half, one, jnp.zeros((heads, head_dim), F32), unroll=4)
    pooled = (total / block_len).astype(BF16)

    def spread(p, carry):
        out_ref[p, heads * ROWS :] = pooled
        return carry

    lax.fori_loop(0, 2 * half, spread, 0, unroll=8)


def pick_kernel(table_ref, parts_ref, out_ref):
    blocks = parts_ref.shape[0]
    base = pl.program_id(0) * blocks * 2

    def one(c, carry):
        out_ref[c, :ROWS] = parts_ref[table_ref[base + 2 * c]]
        out_ref[c, ROWS:] = parts_ref[table_ref[base + 2 * c + 1]]
        return carry

    lax.fori_loop(0, blocks, one, 0, unroll=16)


def halves(x):
    count, rows, head_dim = x.shape
    keys = x[: count // 2].reshape(count // 2 * rows, head_dim)
    values = x[count // 2 :].reshape(count // 2 * rows, head_dim)
    return keys, values


def own_kernel(scale, q_ref, kv_ref, acc_ref, stat_ref):
    keys, values = halves(kv_ref[...])
    scores = lax.dot_general(q_ref[0], keys, ACROSS, preferred_element_type=F32)
    row_ids = lax.broadcasted_iota(jnp.int32, scores.shape, 0)
    col_ids = lax.broadcasted_iota(jnp.int32, scores.shape, 1)
    scores = jnp.where(col_ids <= row_ids, scores, MASKED)
    top = jnp.max(scores, 1, keepdims=True) * scale
    weights = jnp.exp2(scores * scale - top)
    total = jnp.sum(weights, 1, keepdims=True)
    acc_ref[0] = jnp.dot(weights.astype(BF16), values, preferred_element_type=F32)
    lane = lax.broadcasted_iota(jnp.int32, stat_ref.shape[1:], 1)
    stat_ref[0] = jnp.where(lane < stat_ref.shape[2] // 2, top, total)


def give_kernel(scale, q_ref, kv_ref, out_ref, lse_ref):
    keys, values = halves(kv_ref[...])
    scores = lax.dot_general(q_ref[0], keys, ACROSS, preferred_element_type=F32)
    top = jnp.max(scores, 1, keepdims=True) * scale
    weights = jnp.exp2(scores * scale - top)
    total = jnp.sum(weights, 1, keepdims=True)
    acc = jnp.dot(weights.astype(BF16), values, preferred_element_type=F32)
    out_ref[0] = (acc / total).astype(BF16)
    lse_ref[0] = jnp.broadcast_to(top + jnp.log2(total), lse_ref.shape[1:])


def before_kernel(
    scale, given, flag_ref, q_ref, kv_ref, got_ref, lse_ref, acc_ref, stat_ref, acc_out, stat_out
):
    half = stat_ref.shape[2] // 2
    top_before = stat_ref[0][:, :1]
    total_before = stat_ref[0][:, half : half + 1]
    lane = lax.broadcasted_iota(jnp.int32, stat_ref.shape[1:], 1)

    @pl.when(pl.program_id(0) < given)
    def _():
        row = lse_ref[pl.ds(pl.program_id(0), 1)]
        lse = jnp.broadcast_to(row, (stat_ref.shape[2], row.shape[1])).T
        lse = jnp.where(flag_ref[0] > 0, lse, MASKED)
        top = jnp.maximum(lse, top_before)
        share = jnp.exp2(lse - top)
        shrink = jnp.exp2(top_before - top)
        acc_out[0] = got_ref[0].astype(F32) * share + acc_ref[0] * shrink
        stat_out[0] = jnp.where(lane < half, top, total_before * shrink + share)

    @pl.when(pl.program_id(0) >= given)
    def _():
        scores = lax.dot_general(q_ref[0], kv_ref[0, 0], ACROSS, preferred_element_type=F32)
        scores = jnp.where(flag_ref[0] > 0, scores, MASKED)
        top = jnp.maximum(jnp.max(scores, 1, keepdims=True) * scale, top_before)
        weights = jnp.exp2(scores * scale - top)
        shrink = jnp.exp2(top_before - top)
        total = jnp.sum(weights, 1, keepdims=True) + total_before * shrink
        acc = jnp.dot(weights.astype(BF16), kv_ref[1, 0], preferred_element_type=F32)
        acc_out[0] = acc + acc_ref[0] * shrink
        stat_out[0] = jnp.where(lane < half, top, total)


def far_kernel(scale, flag_ref, q_ref, kv_ref, acc_ref, stat_ref, out_ref):
    group, block_len, head_dim = q_ref.shape
    half = stat_ref.shape[2] // 2
    first_head = pl.program_id(0) * group
    step = block_len // 2
    heads = []
    for h in range(group):
        both = [halves(kv_ref[:, (2 * h + s) * ROWS : (2 * h + s + 1) * ROWS]) for s in range(2)]
        keys = jnp.concatenate([both[0][0], both[1][0]], 0)
        values = jnp.concatenate([both[0][1], both[1][1]], 0)
        values = jnp.concatenate([values, jnp.ones_like(values)], 1)
        off = [
            jnp.where(flag_ref[2 * (first_head + h) + s] > 0, 0.0, MASKED) for s in range(2)
        ]
        col = lax.broadcasted_iota(jnp.int32, (1, keys.shape[0]), 1)
        heads.append((keys, values, jnp.where(col < block_len, off[0], off[1])))

    def score(h, start):
        keys, _, off = heads[h]
        q = q_ref[h, start : start + step]
        return lax.dot_general(q, keys, ACROSS, preferred_element_type=F32) + off

    def finish(h, start, scores):
        _, values, _ = heads[h]
        here = pl.ds(start, step)
        stat = stat_ref[h, here]
        top_before = stat[:, :1]
        top = jnp.maximum(jnp.max(scores, 1, keepdims=True) * scale, top_before)
        weights = jnp.exp2(scores * scale - top).astype(BF16)
        shrink = jnp.exp2(top_before - top)
        both = jnp.dot(weights, values, preferred_element_type=F32)
        acc = acc_ref[h, here] * shrink + both[:, :head_dim]
        total = stat[:, half : half + 1] * shrink + both[:, head_dim:]
        out_ref[h, here] = (acc / total).astype(BF16)

    todo = [(h, start) for h in range(group) for start in range(0, block_len, step)]
    scores = score(*todo[0])
    for index, item in enumerate(todo):
        following = score(*todo[index + 1]) if index + 1 < len(todo) else None
        finish(*item, scores)
        scores = following


def body(queries, key_rows, value_rows, selection):
    ctx_size = lax.axis_size("ctx")
    block_len, heads, head_dim = queries.shape
    blocks, _, topk = selection.shape
    assert blocks == ctx_size and topk == 3 and block_len == ROWS * ctx_size // 2
    position = lax.axis_index("ctx")
    scale = LOG2E * head_dim**-0.5
    params = pltpu.CompilerParams(vmem_limit_bytes=58 * 1024 * 1024)
    small = pltpu.CompilerParams(vmem_limit_bytes=32 * 1024 * 1024)

    def cost(matmuls, moved):
        return pl.CostEstimate(
            flops=heads * block_len * block_len * head_dim * 2 * matmuls,
            bytes_accessed=heads * block_len * head_dim * moved,
            transcendentals=heads * block_len * block_len * matmuls // 2,
        )

    whole = pl.BlockSpec((1, block_len, head_dim), lambda h, *_: (h, 0, 0))
    piece = pl.BlockSpec((ctx_size, ROWS, head_dim), lambda h, *_: (0, h, 0))
    pair = pl.BlockSpec((ctx_size, 2 * ROWS, head_dim), lambda h, *_: (0, h, 0))
    by_head = functools.partial(jax.ShapeDtypeStruct, (heads, block_len, head_dim))

    given = 5
    send, q, queries_back, rows_ahead = pl.pallas_call(
        pack_kernel,
        out_shape=[
            jax.ShapeDtypeStruct((ctx_size, heads * (ROWS + 1), head_dim), BF16),
            by_head(BF16),
            jax.ShapeDtypeStruct((given, block_len, head_dim), BF16),
            jax.ShapeDtypeStruct((2, heads - given, block_len, head_dim), BF16),
        ],
        compiler_params=params,
        name="pack",
    )(queries, key_rows, value_rows)
    back = [(i + 1, i) for i in range(ctx_size - 1)]
    ahead = [(i, i + 1) for i in range(ctx_size - 1)]
    next_queries = lax.ppermute(queries_back, "ctx", back)
    rows_before = lax.ppermute(rows_ahead, "ctx", ahead)
    next_queries, rows_before = lax.optimization_barrier((next_queries, rows_before))
    parts = lax.all_to_all(send, "ctx", split_axis=0, concat_axis=0, tiled=True)

    owner = jnp.arange(blocks, dtype=jnp.int32)[:, None]
    first = jnp.where(selection[:, :, 0] == owner - 1, selection[:, :, 1], selection[:, :, 0])
    last = jnp.where(selection[:, :, 2] == owner - 1, selection[:, :, 1], selection[:, :, 2])
    picks = jnp.stack([first, last], axis=2)
    table = picks.transpose(1, 0, 2).reshape(-1)
    mine = lax.dynamic_index_in_dim(picks, position, 0, keepdims=False)
    usable = (mine < position).astype(jnp.int32).reshape(-1)

    gift, gift_lse = pl.pallas_call(
        functools.partial(give_kernel, scale),
        grid=(given,),
        in_specs=[whole, piece],
        out_specs=[whole, whole],
        out_shape=[
            jax.ShapeDtypeStruct((given, block_len, head_dim), BF16),
            jax.ShapeDtypeStruct((given, block_len, head_dim), F32),
        ],
        compiler_params=params,
        cost_estimate=cost(200, 200),
        name="give",
    )(next_queries, send)
    gift_lse = gift_lse[:, :, 0]
    got = lax.ppermute(gift, "ctx", ahead)
    got_lse = lax.ppermute(gift_lse, "ctx", ahead)
    parts, _ = lax.optimization_barrier((parts, gift_lse))

    picked = pl.pallas_call(
        pick_kernel,
        grid_spec=pltpu.PrefetchScalarGridSpec(
            num_scalar_prefetch=1, grid=(heads,), in_specs=[piece], out_specs=pair
        ),
        out_shape=jax.ShapeDtypeStruct((blocks, heads * 2 * ROWS, head_dim), BF16),
        compiler_params=small,
        name="pick",
    )(table, parts)
    fetched = lax.all_to_all(picked, "ctx", split_axis=0, concat_axis=0, tiled=True)

    pooled = parts[:, heads * ROWS :]
    per_head = jnp.einsum("htd,bhd->htb", q, pooled, preferred_element_type=F32)
    causal = jnp.arange(blocks, dtype=jnp.int32) <= position
    affinity = jnp.where(causal, per_head, 0.0).astype(BF16).transpose(1, 0, 2)

    own = pl.pallas_call(
        functools.partial(own_kernel, scale),
        grid=(heads,),
        in_specs=[whole, piece],
        out_specs=[whole, whole],
        out_shape=[by_head(F32), by_head(F32)],
        compiler_params=params,
        cost_estimate=cost(2, 12),
        name="own",
    )(q, send)
    first = pl.BlockSpec(
        (1, block_len, head_dim), lambda h, *_: (jnp.minimum(h, given - 1), 0, 0)
    )
    other = pl.BlockSpec(
        (2, 1, block_len, head_dim), lambda h, *_: (0, jnp.maximum(h - given, 0), 0, 0)
    )
    acc, stat = pl.pallas_call(
        functools.partial(before_kernel, scale, given),
        grid_spec=pltpu.PrefetchScalarGridSpec(
            num_scalar_prefetch=1,
            grid=(heads,),
            in_specs=[whole, other, first, pl.BlockSpec((given, block_len), lambda h, *_: (0, 0)), whole, whole],
            out_specs=[whole, whole],
        ),
        out_shape=[by_head(F32), by_head(F32)],
        compiler_params=params,
        cost_estimate=cost(800, 800),
        name="before",
    )(
        (position > 0).astype(jnp.int32).reshape(1),
        q,
        rows_before,
        got,
        got_lse,
        *own,
    )
    group = 2
    some = pl.BlockSpec((group, block_len, head_dim), lambda h, *_: (h, 0, 0))
    out = pl.pallas_call(
        functools.partial(far_kernel, scale),
        grid_spec=pltpu.PrefetchScalarGridSpec(
            num_scalar_prefetch=1,
            grid=(heads // group,),
            in_specs=[
                some,
                pl.BlockSpec((ctx_size, group * 2 * ROWS, head_dim), lambda h, *_: (0, h, 0)),
                some,
                some,
            ],
            out_specs=some,
        ),
        out_shape=by_head(BF16),
        compiler_params=params,
        cost_estimate=cost(4, 20),
        name="far",
    )(usable, q, fetched, acc, stat)
    return out.transpose(1, 0, 2), affinity


def solution(mesh):
    in_specs = (
        P("ctx", "head", None),
        P("ctx", "head", None),
        P("ctx", "head", None),
        P(None, "head", None),
    )
    out_specs = (P("ctx", "head", None), P("ctx", "head", None))
    return jax.shard_map(body, mesh=mesh, in_specs=in_specs, out_specs=out_specs, check_vma=False)
```

```python
import functools

import jax
import jax.numpy as jnp
from jax import lax
from jax.experimental import pallas as pl
from jax.experimental.pallas import tpu as pltpu
from jax.sharding import PartitionSpec as P

LOG2E = 1.4426950408889634
MASKED = -1e30
ROWS = 16
ACROSS = (((1,), (1,)), ((), ()))
F32 = jnp.float32
BF16 = jnp.bfloat16


def pack_kernel(q_ref, k_ref, v_ref, out_ref, qt_ref, back_ref, ahead_ref, total_ref):
    tokens, heads, head_dim = k_ref.shape
    count = tokens // ROWS
    step, steps = pl.program_id(0), pl.num_programs(0)
    half = count * steps
    given = back_ref.shape[0]

    @pl.when(step == 0)
    def _():
        total_ref[...] = jnp.zeros_like(total_ref)

    def one(p, total):
        here = pl.ds(p * ROWS, ROWS)
        slot = step * count + p
        by_head = jnp.transpose(q_ref[here].astype(F32), (1, 0, 2)).astype(BF16)
        qt_ref[:, here] = by_head
        back_ref[:, here] = by_head[:given]
        keys = k_ref[here].astype(F32)
        by_head = jnp.transpose(keys, (1, 0, 2)).astype(BF16)
        ahead_ref[0, :, here] = by_head[given:]
        out_ref[slot, : heads * ROWS] = by_head.reshape(heads * ROWS, head_dim)
        by_head = jnp.transpose(v_ref[here].astype(F32), (1, 0, 2)).astype(BF16)
        ahead_ref[1, :, here] = by_head[given:]
        out_ref[slot + half, : heads * ROWS] = by_head.reshape(heads * ROWS, head_dim)
        return total + jnp.sum(keys, 0)

    total = total_ref[...]
    for p in range(count):
        total = one(p, total)
    total_ref[...] = total

    @pl.when(step == steps - 1)
    def _():
        pooled = (total / (tokens * steps)).astype(BF16)

        def spread(p, carry):
            out_ref[p, heads * ROWS :] = pooled
            return carry

        lax.fori_loop(0, 2 * half, spread, 0, unroll=8)


def pick_kernel(table_ref, parts_ref, out_ref):
    blocks = parts_ref.shape[0]
    base = pl.program_id(0) * blocks * 2

    def one(c, carry):
        out_ref[c, :ROWS] = parts_ref[table_ref[base + 2 * c]]
        out_ref[c, ROWS:] = parts_ref[table_ref[base + 2 * c + 1]]
        return carry

    lax.fori_loop(0, blocks, one, 0, unroll=16)


def halves(x):
    count, rows, head_dim = x.shape
    keys = x[: count // 2].reshape(count // 2 * rows, head_dim)
    values = x[count // 2 :].reshape(count // 2 * rows, head_dim)
    return keys, values


def own_kernel(scale, q_ref, kv_ref, acc_ref, stat_ref):
    keys, values = halves(kv_ref[...])
    scores = lax.dot_general(q_ref[0], keys, ACROSS, preferred_element_type=F32)
    row_ids = lax.broadcasted_iota(jnp.int32, scores.shape, 0)
    col_ids = lax.broadcasted_iota(jnp.int32, scores.shape, 1)
    scores = jnp.where(col_ids <= row_ids, scores, MASKED)
    top = jnp.max(scores, 1, keepdims=True) * scale
    weights = jnp.exp2(scores * scale - top)
    total = jnp.sum(weights, 1, keepdims=True)
    acc_ref[0] = jnp.dot(weights.astype(BF16), values, preferred_element_type=F32)
    lane = lax.broadcasted_iota(jnp.int32, stat_ref.shape[1:], 1)
    stat_ref[0] = jnp.where(lane < stat_ref.shape[2] // 2, top, total)


def give_kernel(scale, q_ref, kv_ref, out_ref, lse_ref):
    keys, values = halves(kv_ref[...])
    scores = lax.dot_general(q_ref[0], keys, ACROSS, preferred_element_type=F32)
    top = jnp.max(scores, 1, keepdims=True) * scale
    weights = jnp.exp2(scores * scale - top)
    total = jnp.sum(weights, 1, keepdims=True)
    acc = jnp.dot(weights.astype(BF16), values, preferred_element_type=F32)
    out_ref[0] = (acc / total).astype(BF16)
    lse_ref[0] = jnp.broadcast_to(top + jnp.log2(total), lse_ref.shape[1:])


def before_kernel(
    scale, given, flag_ref, q_ref, kv_ref, got_ref, lse_ref, acc_ref, stat_ref, acc_out, lse_out
):
    half = stat_ref.shape[2] // 2
    top_before = stat_ref[0][:, :1]
    total_before = stat_ref[0][:, half : half + 1]

    def put(acc, top, total):
        acc_out[0] = acc / total
        lse = jnp.broadcast_to(top + jnp.log2(total), stat_ref.shape[1:])
        lse_out[0] = lse.T[:1]

    @pl.when(pl.program_id(0) < given)
    def _():
        row = lse_ref[pl.ds(pl.program_id(0), 1)]
        lse = jnp.broadcast_to(row, (stat_ref.shape[2], row.shape[1])).T
        lse = jnp.where(flag_ref[0] > 0, lse, MASKED)
        top = jnp.maximum(lse, top_before)
        share = jnp.exp2(lse - top)
        shrink = jnp.exp2(top_before - top)
        acc = got_ref[0].astype(F32) * share + acc_ref[0] * shrink
        put(acc, top, total_before * shrink + share)

    @pl.when(pl.program_id(0) >= given)
    def _():
        scores = lax.dot_general(q_ref[0], kv_ref[0, 0], ACROSS, preferred_element_type=F32)
        scores = jnp.where(flag_ref[0] > 0, scores, MASKED)
        top = jnp.maximum(jnp.max(scores, 1, keepdims=True) * scale, top_before)
        weights = jnp.exp2(scores * scale - top)
        shrink = jnp.exp2(top_before - top)
        total = jnp.sum(weights, 1, keepdims=True) + total_before * shrink
        acc = jnp.dot(weights.astype(BF16), kv_ref[1, 0], preferred_element_type=F32)
        put(acc + acc_ref[0] * shrink, top, total)


def far_kernel(scale, flag_ref, q_ref, kv_ref, acc_ref, lse_ref, out_ref):
    count, step, head_dim = q_ref.shape

    def score(h):
        keys = jnp.concatenate(
            [halves(kv_ref[:, (2 * h + s) * ROWS : (2 * h + s + 1) * ROWS])[0] for s in range(2)], 0
        )
        off = [jnp.where(flag_ref[2 * h + s] > 0, 0.0, MASKED) for s in range(2)]
        col = lax.broadcasted_iota(jnp.int32, (1, keys.shape[0]), 1)
        scores = lax.dot_general(q_ref[h], keys, ACROSS, preferred_element_type=F32)
        return scores + jnp.where(col < keys.shape[0] // 2, off[0], off[1])

    def finish(h, scores):
        values = jnp.concatenate(
            [halves(kv_ref[:, (2 * h + s) * ROWS : (2 * h + s + 1) * ROWS])[1] for s in range(2)], 0
        )
        values = jnp.concatenate([values, jnp.ones_like(values)], 1)
        lse = jnp.broadcast_to(lse_ref[h : h + 1], (head_dim, step)).T
        top = jnp.maximum(jnp.max(scores, 1, keepdims=True) * scale, lse)
        weights = jnp.exp2(scores * scale - top[:, :1]).astype(BF16)
        share = jnp.exp2(lse - top)
        both = jnp.dot(weights, values, preferred_element_type=F32)
        return (acc_ref[h] * share + both[:, :head_dim]) / (share + both[:, head_dim:])

    results = []
    scores = score(0)
    for h in range(count):
        following = score(h + 1) if h + 1 < count else None
        results.append(finish(h, scores))
        scores = following
    out_ref[...] = jnp.transpose(jnp.stack(results, 0), (1, 0, 2)).astype(BF16)


def body(queries, key_rows, value_rows, selection):
    ctx_size = lax.axis_size("ctx")
    block_len, heads, head_dim = queries.shape
    blocks, _, topk = selection.shape
    assert blocks == ctx_size and topk == 3 and block_len == ROWS * ctx_size // 2
    position = lax.axis_index("ctx")
    scale = LOG2E * head_dim**-0.5
    params = pltpu.CompilerParams(vmem_limit_bytes=58 * 1024 * 1024)
    small = pltpu.CompilerParams(vmem_limit_bytes=32 * 1024 * 1024)

    def cost(matmuls, moved):
        return pl.CostEstimate(
            flops=heads * block_len * block_len * head_dim * 2 * matmuls,
            bytes_accessed=heads * block_len * head_dim * moved,
            transcendentals=heads * block_len * block_len * matmuls // 2,
        )

    whole = pl.BlockSpec((1, block_len, head_dim), lambda h, *_: (h, 0, 0))
    piece = pl.BlockSpec((ctx_size, ROWS, head_dim), lambda h, *_: (0, h, 0))
    pair = pl.BlockSpec((ctx_size, 2 * ROWS, head_dim), lambda h, *_: (0, h, 0))
    by_head = functools.partial(jax.ShapeDtypeStruct, (heads, block_len, head_dim))

    given = 5
    chunks = 4
    tokens = block_len // chunks
    send, q, queries_back, rows_ahead = pl.pallas_call(
        pack_kernel,
        grid=(chunks,),
        in_specs=[pl.BlockSpec((tokens, heads, head_dim), lambda i: (i, 0, 0))] * 3,
        out_specs=[
            pl.BlockSpec((ctx_size, heads * (ROWS + 1), head_dim), lambda i: (0, 0, 0)),
            pl.BlockSpec((heads, tokens, head_dim), lambda i: (0, i, 0)),
            pl.BlockSpec((given, tokens, head_dim), lambda i: (0, i, 0)),
            pl.BlockSpec((2, heads - given, tokens, head_dim), lambda i: (0, 0, i, 0)),
        ],
        scratch_shapes=[pltpu.VMEM((heads, head_dim), F32)],
        out_shape=[
            jax.ShapeDtypeStruct((ctx_size, heads * (ROWS + 1), head_dim), BF16),
            by_head(BF16),
            jax.ShapeDtypeStruct((given, block_len, head_dim), BF16),
            jax.ShapeDtypeStruct((2, heads - given, block_len, head_dim), BF16),
        ],
        compiler_params=params,
        name="pack",
    )(queries, key_rows, value_rows)
    back = [(i + 1, i) for i in range(ctx_size - 1)]
    ahead = [(i, i + 1) for i in range(ctx_size - 1)]
    next_queries = lax.ppermute(queries_back, "ctx", back)
    rows_before = lax.ppermute(rows_ahead, "ctx", ahead)
    next_queries, rows_before = lax.optimization_barrier((next_queries, rows_before))
    parts = lax.all_to_all(send, "ctx", split_axis=0, concat_axis=0, tiled=True)

    owner = jnp.arange(blocks, dtype=jnp.int32)[:, None]
    first = jnp.where(selection[:, :, 0] == owner - 1, selection[:, :, 1], selection[:, :, 0])
    last = jnp.where(selection[:, :, 2] == owner - 1, selection[:, :, 1], selection[:, :, 2])
    picks = jnp.stack([first, last], axis=2)
    table = picks.transpose(1, 0, 2).reshape(-1)
    mine = lax.dynamic_index_in_dim(picks, position, 0, keepdims=False)
    usable = (mine < position).astype(jnp.int32).reshape(-1)

    gift, gift_lse = pl.pallas_call(
        functools.partial(give_kernel, scale),
        grid=(given,),
        in_specs=[whole, piece],
        out_specs=[whole, whole],
        out_shape=[
            jax.ShapeDtypeStruct((given, block_len, head_dim), BF16),
            jax.ShapeDtypeStruct((given, block_len, head_dim), F32),
        ],
        compiler_params=params,
        cost_estimate=cost(200, 200),
        name="give",
    )(next_queries, send)
    gift_lse = gift_lse[:, :, 0]
    got = lax.ppermute(gift, "ctx", ahead)
    got_lse = lax.ppermute(gift_lse, "ctx", ahead)
    parts, _ = lax.optimization_barrier((parts, gift_lse))

    picked = pl.pallas_call(
        pick_kernel,
        grid_spec=pltpu.PrefetchScalarGridSpec(
            num_scalar_prefetch=1, grid=(heads,), in_specs=[piece], out_specs=pair
        ),
        out_shape=jax.ShapeDtypeStruct((blocks, heads * 2 * ROWS, head_dim), BF16),
        compiler_params=small,
        name="pick",
    )(table, parts)
    fetched = lax.all_to_all(picked, "ctx", split_axis=0, concat_axis=0, tiled=True)

    pooled = parts[:, heads * ROWS :]
    per_head = jnp.einsum("htd,bhd->htb", q, pooled, preferred_element_type=F32)
    causal = jnp.arange(blocks, dtype=jnp.int32) <= position
    affinity = jnp.where(causal, per_head, 0.0).astype(BF16).transpose(1, 0, 2)

    own = pl.pallas_call(
        functools.partial(own_kernel, scale),
        grid=(heads,),
        in_specs=[whole, piece],
        out_specs=[whole, whole],
        out_shape=[by_head(F32), by_head(F32)],
        compiler_params=params,
        cost_estimate=cost(2, 12),
        name="own",
    )(q, send)
    first = pl.BlockSpec(
        (1, block_len, head_dim), lambda h, *_: (jnp.minimum(h, given - 1), 0, 0)
    )
    other = pl.BlockSpec(
        (2, 1, block_len, head_dim), lambda h, *_: (0, jnp.maximum(h - given, 0), 0, 0)
    )
    acc, lse = pl.pallas_call(
        functools.partial(before_kernel, scale, given),
        grid_spec=pltpu.PrefetchScalarGridSpec(
            num_scalar_prefetch=1,
            grid=(heads,),
            in_specs=[whole, other, first, pl.BlockSpec((given, block_len), lambda h, *_: (0, 0)), whole, whole],
            out_specs=[whole, pl.BlockSpec((1, 1, block_len), lambda h, *_: (h, 0, 0))],
        ),
        out_shape=[by_head(F32), jax.ShapeDtypeStruct((heads, 1, block_len), F32)],
        compiler_params=params,
        cost_estimate=cost(800, 800),
        name="before",
    )(
        (position > 0).astype(jnp.int32).reshape(1),
        q,
        rows_before,
        got,
        got_lse,
        *own,
    )
    step = block_len // 2
    some = pl.BlockSpec((heads, step, head_dim), lambda i, *_: (0, i, 0))
    attended = pl.pallas_call(
        functools.partial(far_kernel, scale),
        grid_spec=pltpu.PrefetchScalarGridSpec(
            num_scalar_prefetch=1,
            grid=(block_len // step,),
            in_specs=[
                some,
                pl.BlockSpec((ctx_size, heads * 2 * ROWS, head_dim), lambda i, *_: (0, 0, 0)),
                some,
                pl.BlockSpec((heads, step), lambda i, *_: (0, i)),
            ],
            out_specs=pl.BlockSpec((step, heads, head_dim), lambda i, *_: (i, 0, 0)),
        ),
        out_shape=jax.ShapeDtypeStruct((block_len, heads, head_dim), BF16),
        compiler_params=params,
        cost_estimate=cost(4, 20),
        name="far",
    )(usable, q, fetched, acc, lse[:, 0])
    return attended, affinity


def solution(mesh):
    in_specs = (
        P("ctx", "head", None),
        P("ctx", "head", None),
        P("ctx", "head", None),
        P(None, "head", None),
    )
    out_specs = (P("ctx", "head", None), P("ctx", "head", None))
    return jax.shard_map(body, mesh=mesh, in_specs=in_specs, out_specs=out_specs, check_vma=False)
```

```python
import functools

import jax
import jax.numpy as jnp
from jax import lax
from jax.experimental import pallas as pl
from jax.experimental.pallas import tpu as pltpu
from jax.sharding import PartitionSpec as P

LOG2E = 1.4426950408889634
MASKED = -1e30
ROWS = 16
ACROSS = (((1,), (1,)), ((), ()))
F32 = jnp.float32
BF16 = jnp.bfloat16


def pack_kernel(q_ref, k_ref, v_ref, out_ref, qt_ref, back_ref, ahead_ref, total_ref):
    tokens, heads, head_dim = k_ref.shape
    count = tokens // ROWS
    step, steps = pl.program_id(0), pl.num_programs(0)
    half = count * steps
    given = back_ref.shape[0]

    @pl.when(step == 0)
    def _():
        total_ref[...] = jnp.zeros_like(total_ref)

    def one(p, total):
        here = pl.ds(p * ROWS, ROWS)
        slot = step * count + p
        by_head = jnp.transpose(q_ref[here].astype(F32), (1, 0, 2)).astype(BF16)
        qt_ref[:, here] = by_head
        back_ref[:, here] = by_head[:given]
        keys = k_ref[here].astype(F32)
        by_head = jnp.transpose(keys, (1, 0, 2)).astype(BF16)
        ahead_ref[0, :, here] = by_head[given:]
        out_ref[slot, : heads * ROWS] = by_head.reshape(heads * ROWS, head_dim)
        by_head = jnp.transpose(v_ref[here].astype(F32), (1, 0, 2)).astype(BF16)
        ahead_ref[1, :, here] = by_head[given:]
        out_ref[slot + half, : heads * ROWS] = by_head.reshape(heads * ROWS, head_dim)
        return total + jnp.sum(keys, 0)

    total = total_ref[...]
    for p in range(count):
        total = one(p, total)
    total_ref[...] = total

    @pl.when(step == steps - 1)
    def _():
        pooled = (total / (tokens * steps)).astype(BF16)

        def spread(p, carry):
            out_ref[p, heads * ROWS :] = pooled
            return carry

        lax.fori_loop(0, 2 * half, spread, 0, unroll=8)


def pick_kernel(table_ref, parts_ref, out_ref):
    count, rows, _ = out_ref.shape
    base = pl.program_id(0) * count * (rows // ROWS)

    def one(c, carry):
        for item in range(rows // ROWS):
            here = pl.ds(item // 2 * ROWS, ROWS)
            picked = table_ref[base + c * (rows // ROWS) + item]
            out_ref[c, item * ROWS : (item + 1) * ROWS] = parts_ref[picked, here]
        return carry

    lax.fori_loop(0, count, one, 0, unroll=True)


def halves(x):
    count, rows, head_dim = x.shape
    keys = x[: count // 2].reshape(count // 2 * rows, head_dim)
    values = x[count // 2 :].reshape(count // 2 * rows, head_dim)
    return keys, values


def own_kernel(scale, q_ref, kv_ref, acc_ref, stat_ref):
    keys, values = halves(kv_ref[...])
    scores = lax.dot_general(q_ref[0], keys, ACROSS, preferred_element_type=F32)
    row_ids = lax.broadcasted_iota(jnp.int32, scores.shape, 0)
    col_ids = lax.broadcasted_iota(jnp.int32, scores.shape, 1)
    scores = jnp.where(col_ids <= row_ids, scores, MASKED)
    top = jnp.max(scores, 1, keepdims=True) * scale
    weights = jnp.exp2(scores * scale - top)
    total = jnp.sum(weights, 1, keepdims=True)
    acc_ref[0] = jnp.dot(weights.astype(BF16), values, preferred_element_type=F32)
    lane = lax.broadcasted_iota(jnp.int32, stat_ref.shape[1:], 1)
    stat_ref[0] = jnp.where(lane < stat_ref.shape[2] // 2, top, total)


def give_kernel(scale, q_ref, kv_ref, out_ref, lse_ref):
    keys, values = halves(kv_ref[...])
    scores = lax.dot_general(q_ref[0], keys, ACROSS, preferred_element_type=F32)
    top = jnp.max(scores, 1, keepdims=True) * scale
    weights = jnp.exp2(scores * scale - top)
    total = jnp.sum(weights, 1, keepdims=True)
    acc = jnp.dot(weights.astype(BF16), values, preferred_element_type=F32)
    out_ref[0] = (acc / total).astype(BF16)
    lse_ref[0] = jnp.broadcast_to(top + jnp.log2(total), lse_ref.shape[1:])


def before_kernel(
    scale, given, flag_ref, q_ref, kv_ref, got_ref, lse_ref, acc_ref, stat_ref, acc_out, lse_out
):
    half = stat_ref.shape[2] // 2
    top_before = stat_ref[0][:, :1]
    total_before = stat_ref[0][:, half : half + 1]

    def put(acc, top, total):
        acc_out[0] = acc / total
        lse = jnp.broadcast_to(top + jnp.log2(total), stat_ref.shape[1:])
        lse_out[0] = lse.T[:1]

    @pl.when(pl.program_id(0) < given)
    def _():
        row = lse_ref[pl.ds(pl.program_id(0), 1)]
        lse = jnp.broadcast_to(row, (stat_ref.shape[2], row.shape[1])).T
        lse = jnp.where(flag_ref[0] > 0, lse, MASKED)
        top = jnp.maximum(lse, top_before)
        share = jnp.exp2(lse - top)
        shrink = jnp.exp2(top_before - top)
        acc = got_ref[0].astype(F32) * share + acc_ref[0] * shrink
        put(acc, top, total_before * shrink + share)

    @pl.when(pl.program_id(0) >= given)
    def _():
        scores = lax.dot_general(q_ref[0], kv_ref[0, 0], ACROSS, preferred_element_type=F32)
        scores = jnp.where(flag_ref[0] > 0, scores, MASKED)
        top = jnp.maximum(jnp.max(scores, 1, keepdims=True) * scale, top_before)
        weights = jnp.exp2(scores * scale - top)
        shrink = jnp.exp2(top_before - top)
        total = jnp.sum(weights, 1, keepdims=True) + total_before * shrink
        acc = jnp.dot(weights.astype(BF16), kv_ref[1, 0], preferred_element_type=F32)
        put(acc + acc_ref[0] * shrink, top, total)


def far_kernel(scale, flag_ref, q_ref, kv_ref, acc_ref, lse_ref, out_ref):
    count, step, head_dim = q_ref.shape

    def score(h):
        keys = jnp.concatenate(
            [halves(kv_ref[:, (2 * h + s) * ROWS : (2 * h + s + 1) * ROWS])[0] for s in range(2)], 0
        )
        off = [jnp.where(flag_ref[2 * h + s] > 0, 0.0, MASKED) for s in range(2)]
        col = lax.broadcasted_iota(jnp.int32, (1, keys.shape[0]), 1)
        scores = lax.dot_general(q_ref[h], keys, ACROSS, preferred_element_type=F32)
        return scores + jnp.where(col < keys.shape[0] // 2, off[0], off[1])

    def finish(h, scores):
        values = jnp.concatenate(
            [halves(kv_ref[:, (2 * h + s) * ROWS : (2 * h + s + 1) * ROWS])[1] for s in range(2)], 0
        )
        values = jnp.concatenate([values, jnp.ones_like(values)], 1)
        lse = jnp.broadcast_to(lse_ref[h : h + 1], (head_dim, step)).T
        top = jnp.maximum(jnp.max(scores, 1, keepdims=True) * scale, lse)
        weights = jnp.exp2(scores * scale - top[:, :1]).astype(BF16)
        share = jnp.exp2(lse - top)
        both = jnp.dot(weights, values, preferred_element_type=F32)
        return (acc_ref[h] * share + both[:, :head_dim]) / (share + both[:, head_dim:])

    results = []
    scores = score(0)
    for h in range(count):
        following = score(h + 1) if h + 1 < count else None
        results.append(finish(h, scores))
        scores = following
    out_ref[...] = jnp.transpose(jnp.stack(results, 0), (1, 0, 2)).astype(BF16)


def body(queries, key_rows, value_rows, selection):
    ctx_size = lax.axis_size("ctx")
    block_len, heads, head_dim = queries.shape
    blocks, _, topk = selection.shape
    assert blocks == ctx_size and topk == 3 and block_len == ROWS * ctx_size // 2
    position = lax.axis_index("ctx")
    scale = LOG2E * head_dim**-0.5
    params = pltpu.CompilerParams(vmem_limit_bytes=58 * 1024 * 1024)
    small = pltpu.CompilerParams(vmem_limit_bytes=32 * 1024 * 1024)

    def cost(matmuls, moved):
        return pl.CostEstimate(
            flops=heads * block_len * block_len * head_dim * 2 * matmuls,
            bytes_accessed=heads * block_len * head_dim * moved,
            transcendentals=heads * block_len * block_len * matmuls // 2,
        )

    whole = pl.BlockSpec((1, block_len, head_dim), lambda h, *_: (h, 0, 0))
    piece = pl.BlockSpec((ctx_size, ROWS, head_dim), lambda h, *_: (0, h, 0))
    pair = pl.BlockSpec((ctx_size, 2 * ROWS, head_dim), lambda h, *_: (0, h, 0))
    by_head = functools.partial(jax.ShapeDtypeStruct, (heads, block_len, head_dim))

    given = 5
    chunks = 2
    tokens = block_len // chunks
    send, q, queries_back, rows_ahead = pl.pallas_call(
        pack_kernel,
        grid=(chunks,),
        in_specs=[pl.BlockSpec((tokens, heads, head_dim), lambda i: (i, 0, 0))] * 3,
        out_specs=[
            pl.BlockSpec((ctx_size, heads * (ROWS + 1), head_dim), lambda i: (0, 0, 0)),
            pl.BlockSpec((heads, tokens, head_dim), lambda i: (0, i, 0)),
            pl.BlockSpec((given, tokens, head_dim), lambda i: (0, i, 0)),
            pl.BlockSpec((2, heads - given, tokens, head_dim), lambda i: (0, 0, i, 0)),
        ],
        scratch_shapes=[pltpu.VMEM((heads, head_dim), F32)],
        out_shape=[
            jax.ShapeDtypeStruct((ctx_size, heads * (ROWS + 1), head_dim), BF16),
            by_head(BF16),
            jax.ShapeDtypeStruct((given, block_len, head_dim), BF16),
            jax.ShapeDtypeStruct((2, heads - given, block_len, head_dim), BF16),
        ],
        compiler_params=params,
        name="pack",
    )(queries, key_rows, value_rows)
    back = [(i + 1, i) for i in range(ctx_size - 1)]
    ahead = [(i, i + 1) for i in range(ctx_size - 1)]
    next_queries = lax.ppermute(queries_back, "ctx", back)
    rows_before = lax.ppermute(rows_ahead, "ctx", ahead)
    next_queries, rows_before = lax.optimization_barrier((next_queries, rows_before))
    parts = lax.all_to_all(send, "ctx", split_axis=0, concat_axis=0, tiled=True)

    owner = jnp.arange(blocks, dtype=jnp.int32)[:, None]
    first = jnp.where(selection[:, :, 0] == owner - 1, selection[:, :, 1], selection[:, :, 0])
    last = jnp.where(selection[:, :, 2] == owner - 1, selection[:, :, 1], selection[:, :, 2])
    picks = jnp.stack([first, last], axis=2)
    table = picks.reshape(-1)
    mine = lax.dynamic_index_in_dim(picks, position, 0, keepdims=False)
    usable = (mine < position).astype(jnp.int32).reshape(-1)

    gift, gift_lse = pl.pallas_call(
        functools.partial(give_kernel, scale),
        grid=(given,),
        in_specs=[whole, piece],
        out_specs=[whole, whole],
        out_shape=[
            jax.ShapeDtypeStruct((given, block_len, head_dim), BF16),
            jax.ShapeDtypeStruct((given, block_len, head_dim), F32),
        ],
        compiler_params=params,
        cost_estimate=cost(200, 200),
        name="give",
    )(next_queries, send)
    gift_lse = gift_lse[:, :, 0]
    got = lax.ppermute(gift, "ctx", ahead)
    got_lse = lax.ppermute(gift_lse, "ctx", ahead)
    parts, _ = lax.optimization_barrier((parts, gift_lse))

    some = blocks // 8
    picked = pl.pallas_call(
        pick_kernel,
        grid_spec=pltpu.PrefetchScalarGridSpec(
            num_scalar_prefetch=1,
            grid=(blocks // some,),
            in_specs=[pl.BlockSpec(send.shape, lambda i, *_: (0, 0, 0))],
            out_specs=pl.BlockSpec((some, heads * 2 * ROWS, head_dim), lambda i, *_: (i, 0, 0)),
        ),
        out_shape=pltpu.HBM((blocks, heads * 2 * ROWS, head_dim), BF16),
        compiler_params=small,
        name="pick",
    )(table, parts)
    fetched = lax.all_to_all(picked, "ctx", split_axis=0, concat_axis=0, tiled=True)

    pooled = parts[:, heads * ROWS :]
    per_head = jnp.einsum("htd,bhd->htb", q, pooled, preferred_element_type=F32)
    causal = jnp.arange(blocks, dtype=jnp.int32) <= position
    affinity = jnp.where(causal, per_head, 0.0).astype(BF16).transpose(1, 0, 2)

    own = pl.pallas_call(
        functools.partial(own_kernel, scale),
        grid=(heads,),
        in_specs=[whole, piece],
        out_specs=[whole, whole],
        out_shape=[by_head(F32), by_head(F32)],
        compiler_params=params,
        cost_estimate=cost(2, 12),
        name="own",
    )(q, send)
    first = pl.BlockSpec(
        (1, block_len, head_dim), lambda h, *_: (jnp.minimum(h, given - 1), 0, 0)
    )
    other = pl.BlockSpec(
        (2, 1, block_len, head_dim), lambda h, *_: (0, jnp.maximum(h - given, 0), 0, 0)
    )
    acc, lse = pl.pallas_call(
        functools.partial(before_kernel, scale, given),
        grid_spec=pltpu.PrefetchScalarGridSpec(
            num_scalar_prefetch=1,
            grid=(heads,),
            in_specs=[whole, other, first, pl.BlockSpec((given, block_len), lambda h, *_: (0, 0)), whole, whole],
            out_specs=[whole, pl.BlockSpec((1, 1, block_len), lambda h, *_: (h, 0, 0))],
        ),
        out_shape=[by_head(F32), jax.ShapeDtypeStruct((heads, 1, block_len), F32)],
        compiler_params=params,
        cost_estimate=cost(800, 800),
        name="before",
    )(
        (position > 0).astype(jnp.int32).reshape(1),
        q,
        rows_before,
        got,
        got_lse,
        *own,
    )
    step = block_len // 2
    some = pl.BlockSpec((heads, step, head_dim), lambda i, *_: (0, i, 0))
    attended = pl.pallas_call(
        functools.partial(far_kernel, scale),
        grid_spec=pltpu.PrefetchScalarGridSpec(
            num_scalar_prefetch=1,
            grid=(block_len // step,),
            in_specs=[
                some,
                pl.BlockSpec((ctx_size, heads * 2 * ROWS, head_dim), lambda i, *_: (0, 0, 0)),
                some,
                pl.BlockSpec((heads, step), lambda i, *_: (0, i)),
            ],
            out_specs=pl.BlockSpec((step, heads, head_dim), lambda i, *_: (i, 0, 0)),
        ),
        out_shape=jax.ShapeDtypeStruct((block_len, heads, head_dim), BF16),
        compiler_params=params,
        cost_estimate=cost(4, 20),
        name="far",
    )(usable, q, fetched, acc, lse[:, 0])
    return attended, affinity


def solution(mesh):
    in_specs = (
        P("ctx", "head", None),
        P("ctx", "head", None),
        P("ctx", "head", None),
        P(None, "head", None),
    )
    out_specs = (P("ctx", "head", None), P("ctx", "head", None))
    return jax.shard_map(body, mesh=mesh, in_specs=in_specs, out_specs=out_specs, check_vma=False)
```

```python
import functools

import jax
import jax.numpy as jnp
from jax import lax
from jax.experimental import pallas as pl
from jax.experimental.pallas import tpu as pltpu
from jax.sharding import PartitionSpec as P

LOG2E = 1.4426950408889634
MASKED = -1e30
ROWS = 16
ACROSS = (((1,), (1,)), ((), ()))
F32 = jnp.float32
BF16 = jnp.bfloat16


def pack_kernel(q_ref, k_ref, v_ref, out_ref, back_ref, ahead_ref, total_ref):
    tokens, heads, head_dim = k_ref.shape
    count = tokens // ROWS
    step, steps = pl.program_id(0), pl.num_programs(0)
    half = count * steps
    given = back_ref.shape[0]

    @pl.when(step == 0)
    def _():
        total_ref[...] = jnp.zeros_like(total_ref)

    def one(p, total):
        here = pl.ds(p * ROWS, ROWS)
        slot = step * count + p
        by_head = jnp.transpose(q_ref[here].astype(F32), (1, 0, 2)).astype(BF16)
        back_ref[:, here] = by_head[:given]
        keys = k_ref[here].astype(F32)
        by_head = jnp.transpose(keys, (1, 0, 2)).astype(BF16)
        ahead_ref[0, :, here] = by_head[given:]
        out_ref[slot, : heads * ROWS] = by_head.reshape(heads * ROWS, head_dim)
        by_head = jnp.transpose(v_ref[here].astype(F32), (1, 0, 2)).astype(BF16)
        ahead_ref[1, :, here] = by_head[given:]
        out_ref[slot + half, : heads * ROWS] = by_head.reshape(heads * ROWS, head_dim)
        return total + jnp.sum(keys, 0)

    total = total_ref[...]
    for p in range(count):
        total = one(p, total)
    total_ref[...] = total

    @pl.when(step == steps - 1)
    def _():
        pooled = (total / (tokens * steps)).astype(BF16)

        def spread(p, carry):
            out_ref[p, heads * ROWS :] = pooled
            return carry

        lax.fori_loop(0, 2 * half, spread, 0, unroll=8)


def pick_kernel(table_ref, parts_ref, out_ref):
    count, rows, _ = out_ref.shape
    base = pl.program_id(0) * count * (rows // ROWS)

    def one(c, carry):
        for item in range(rows // ROWS):
            here = pl.ds(item // 2 * ROWS, ROWS)
            picked = table_ref[base + c * (rows // ROWS) + item]
            out_ref[c, item * ROWS : (item + 1) * ROWS] = parts_ref[picked, here]
        return carry

    lax.fori_loop(0, count, one, 0, unroll=True)


def halves(x):
    count, rows, head_dim = x.shape
    keys = x[: count // 2].reshape(count // 2 * rows, head_dim)
    values = x[count // 2 :].reshape(count // 2 * rows, head_dim)
    return keys, values


def own_kernel(scale, q_ref, kv_ref, acc_ref, stat_ref):
    keys, values = halves(kv_ref[...])
    scores = lax.dot_general(q_ref[0], keys, ACROSS, preferred_element_type=F32)
    row_ids = lax.broadcasted_iota(jnp.int32, scores.shape, 0)
    col_ids = lax.broadcasted_iota(jnp.int32, scores.shape, 1)
    scores = jnp.where(col_ids <= row_ids, scores, MASKED)
    top = jnp.max(scores, 1, keepdims=True) * scale
    weights = jnp.exp2(scores * scale - top)
    total = jnp.sum(weights, 1, keepdims=True)
    acc_ref[0] = jnp.dot(weights.astype(BF16), values, preferred_element_type=F32)
    lane = lax.broadcasted_iota(jnp.int32, stat_ref.shape[1:], 1)
    stat_ref[0] = jnp.where(lane < stat_ref.shape[2] // 2, top, total)


def give_kernel(scale, q_ref, kv_ref, out_ref, lse_ref):
    keys, values = halves(kv_ref[...])
    scores = lax.dot_general(q_ref[0], keys, ACROSS, preferred_element_type=F32)
    top = jnp.max(scores, 1, keepdims=True) * scale
    weights = jnp.exp2(scores * scale - top)
    total = jnp.sum(weights, 1, keepdims=True)
    acc = jnp.dot(weights.astype(BF16), values, preferred_element_type=F32)
    out_ref[0] = (acc / total).astype(BF16)
    lse_ref[0] = jnp.broadcast_to(top + jnp.log2(total), lse_ref.shape[1:])


def before_kernel(
    scale, given, flag_ref, q_ref, kv_ref, got_ref, lse_ref, acc_ref, stat_ref, acc_out, lse_out
):
    half = stat_ref.shape[2] // 2
    top_before = stat_ref[0][:, :1]
    total_before = stat_ref[0][:, half : half + 1]

    def put(acc, top, total):
        acc_out[0] = acc / total
        lse = jnp.broadcast_to(top + jnp.log2(total), stat_ref.shape[1:])
        lse_out[0] = lse.T[:1]

    @pl.when(pl.program_id(0) < given)
    def _():
        row = lse_ref[pl.ds(pl.program_id(0), 1)]
        lse = jnp.broadcast_to(row, (stat_ref.shape[2], row.shape[1])).T
        lse = jnp.where(flag_ref[0] > 0, lse, MASKED)
        top = jnp.maximum(lse, top_before)
        share = jnp.exp2(lse - top)
        shrink = jnp.exp2(top_before - top)
        acc = got_ref[0].astype(F32) * share + acc_ref[0] * shrink
        put(acc, top, total_before * shrink + share)

    @pl.when(pl.program_id(0) >= given)
    def _():
        scores = lax.dot_general(q_ref[0], kv_ref[0, 0], ACROSS, preferred_element_type=F32)
        scores = jnp.where(flag_ref[0] > 0, scores, MASKED)
        top = jnp.maximum(jnp.max(scores, 1, keepdims=True) * scale, top_before)
        weights = jnp.exp2(scores * scale - top)
        shrink = jnp.exp2(top_before - top)
        total = jnp.sum(weights, 1, keepdims=True) + total_before * shrink
        acc = jnp.dot(weights.astype(BF16), kv_ref[1, 0], preferred_element_type=F32)
        put(acc + acc_ref[0] * shrink, top, total)


def far_kernel(scale, flag_ref, q_ref, kv_ref, acc_ref, lse_ref, out_ref):
    count, step, head_dim = q_ref.shape

    def score(h):
        keys = jnp.concatenate(
            [halves(kv_ref[:, (2 * h + s) * ROWS : (2 * h + s + 1) * ROWS])[0] for s in range(2)], 0
        )
        off = [jnp.where(flag_ref[2 * h + s] > 0, 0.0, MASKED) for s in range(2)]
        col = lax.broadcasted_iota(jnp.int32, (1, keys.shape[0]), 1)
        scores = lax.dot_general(q_ref[h], keys, ACROSS, preferred_element_type=F32)
        return scores + jnp.where(col < keys.shape[0] // 2, off[0], off[1])

    def finish(h, scores):
        values = jnp.concatenate(
            [halves(kv_ref[:, (2 * h + s) * ROWS : (2 * h + s + 1) * ROWS])[1] for s in range(2)], 0
        )
        values = jnp.concatenate([values, jnp.ones_like(values)], 1)
        lse = jnp.broadcast_to(lse_ref[h : h + 1], (head_dim, step)).T
        top = jnp.maximum(jnp.max(scores, 1, keepdims=True) * scale, lse)
        weights = jnp.exp2(scores * scale - top[:, :1]).astype(BF16)
        share = jnp.exp2(lse - top)
        both = jnp.dot(weights, values, preferred_element_type=F32)
        return (acc_ref[h] * share + both[:, :head_dim]) / (share + both[:, head_dim:])

    results = []
    scores = score(0)
    for h in range(count):
        following = score(h + 1) if h + 1 < count else None
        results.append(finish(h, scores))
        scores = following
    out_ref[...] = jnp.transpose(jnp.stack(results, 0), (1, 0, 2)).astype(BF16)


def body(queries, key_rows, value_rows, selection):
    ctx_size = lax.axis_size("ctx")
    block_len, heads, head_dim = queries.shape
    blocks, _, topk = selection.shape
    assert blocks == ctx_size and topk == 3 and block_len == ROWS * ctx_size // 2
    position = lax.axis_index("ctx")
    scale = LOG2E * head_dim**-0.5
    params = pltpu.CompilerParams(vmem_limit_bytes=58 * 1024 * 1024)
    small = pltpu.CompilerParams(vmem_limit_bytes=32 * 1024 * 1024)

    def cost(matmuls, moved):
        return pl.CostEstimate(
            flops=heads * block_len * block_len * head_dim * 2 * matmuls,
            bytes_accessed=heads * block_len * head_dim * moved,
            transcendentals=heads * block_len * block_len * matmuls // 2,
        )

    whole = pl.BlockSpec((1, block_len, head_dim), lambda h, *_: (h, 0, 0))
    piece = pl.BlockSpec((ctx_size, ROWS, head_dim), lambda h, *_: (0, h, 0))
    pair = pl.BlockSpec((ctx_size, 2 * ROWS, head_dim), lambda h, *_: (0, h, 0))
    by_head = functools.partial(jax.ShapeDtypeStruct, (heads, block_len, head_dim))

    given = 5
    chunks = 2
    tokens = block_len // chunks
    send, queries_back, rows_ahead = pl.pallas_call(
        pack_kernel,
        grid=(chunks,),
        in_specs=[pl.BlockSpec((tokens, heads, head_dim), lambda i: (i, 0, 0))] * 3,
        out_specs=[
            pl.BlockSpec((ctx_size, heads * (ROWS + 1), head_dim), lambda i: (0, 0, 0)),
            pl.BlockSpec((given, tokens, head_dim), lambda i: (0, i, 0)),
            pl.BlockSpec((2, heads - given, tokens, head_dim), lambda i: (0, 0, i, 0)),
        ],
        scratch_shapes=[pltpu.VMEM((heads, head_dim), F32)],
        out_shape=[
            jax.ShapeDtypeStruct((ctx_size, heads * (ROWS + 1), head_dim), BF16),
            jax.ShapeDtypeStruct((given, block_len, head_dim), BF16),
            jax.ShapeDtypeStruct((2, heads - given, block_len, head_dim), BF16),
        ],
        compiler_params=params,
        name="pack",
    )(queries, key_rows, value_rows)
    q = queries.transpose(1, 0, 2)
    back = [(i + 1, i) for i in range(ctx_size - 1)]
    ahead = [(i, i + 1) for i in range(ctx_size - 1)]
    next_queries = lax.ppermute(queries_back, "ctx", back)
    rows_before = lax.ppermute(rows_ahead, "ctx", ahead)
    next_queries, rows_before = lax.optimization_barrier((next_queries, rows_before))
    parts = lax.all_to_all(send, "ctx", split_axis=0, concat_axis=0, tiled=True)

    owner = jnp.arange(blocks, dtype=jnp.int32)[:, None]
    first = jnp.where(selection[:, :, 0] == owner - 1, selection[:, :, 1], selection[:, :, 0])
    last = jnp.where(selection[:, :, 2] == owner - 1, selection[:, :, 1], selection[:, :, 2])
    picks = jnp.stack([first, last], axis=2)
    table = picks.reshape(-1)
    mine = lax.dynamic_index_in_dim(picks, position, 0, keepdims=False)
    usable = (mine < position).astype(jnp.int32).reshape(-1)

    gift, gift_lse = pl.pallas_call(
        functools.partial(give_kernel, scale),
        grid=(given,),
        in_specs=[whole, piece],
        out_specs=[whole, whole],
        out_shape=[
            jax.ShapeDtypeStruct((given, block_len, head_dim), BF16),
            jax.ShapeDtypeStruct((given, block_len, head_dim), F32),
        ],
        compiler_params=params,
        cost_estimate=cost(200, 200),
        name="give",
    )(next_queries, send)
    gift_lse = gift_lse[:, :, 0]
    got = lax.ppermute(gift, "ctx", ahead)
    got_lse = lax.ppermute(gift_lse, "ctx", ahead)
    parts, _ = lax.optimization_barrier((parts, gift_lse))

    some = blocks // 8
    picked = pl.pallas_call(
        pick_kernel,
        grid_spec=pltpu.PrefetchScalarGridSpec(
            num_scalar_prefetch=1,
            grid=(blocks // some,),
            in_specs=[pl.BlockSpec(send.shape, lambda i, *_: (0, 0, 0))],
            out_specs=pl.BlockSpec((some, heads * 2 * ROWS, head_dim), lambda i, *_: (i, 0, 0)),
        ),
        out_shape=pltpu.HBM((blocks, heads * 2 * ROWS, head_dim), BF16),
        compiler_params=small,
        name="pick",
    )(table, parts)
    fetched = lax.all_to_all(picked, "ctx", split_axis=0, concat_axis=0, tiled=True)

    pooled = parts[:, heads * ROWS :]
    per_head = jnp.einsum("htd,bhd->htb", q, pooled, preferred_element_type=F32)
    causal = jnp.arange(blocks, dtype=jnp.int32) <= position
    affinity = jnp.where(causal, per_head, 0.0).astype(BF16).transpose(1, 0, 2)

    own = pl.pallas_call(
        functools.partial(own_kernel, scale),
        grid=(heads,),
        in_specs=[whole, piece],
        out_specs=[whole, whole],
        out_shape=[by_head(F32), by_head(F32)],
        compiler_params=params,
        cost_estimate=cost(2, 12),
        name="own",
    )(q, send)
    first = pl.BlockSpec(
        (1, block_len, head_dim), lambda h, *_: (jnp.minimum(h, given - 1), 0, 0)
    )
    other = pl.BlockSpec(
        (2, 1, block_len, head_dim), lambda h, *_: (0, jnp.maximum(h - given, 0), 0, 0)
    )
    acc, lse = pl.pallas_call(
        functools.partial(before_kernel, scale, given),
        grid_spec=pltpu.PrefetchScalarGridSpec(
            num_scalar_prefetch=1,
            grid=(heads,),
            in_specs=[whole, other, first, pl.BlockSpec((given, block_len), lambda h, *_: (0, 0)), whole, whole],
            out_specs=[whole, pl.BlockSpec((1, 1, block_len), lambda h, *_: (h, 0, 0))],
        ),
        out_shape=[by_head(F32), jax.ShapeDtypeStruct((heads, 1, block_len), F32)],
        compiler_params=params,
        cost_estimate=cost(800, 800),
        name="before",
    )(
        (position > 0).astype(jnp.int32).reshape(1),
        q,
        rows_before,
        got,
        got_lse,
        *own,
    )
    step = block_len // 2
    some = pl.BlockSpec((heads, step, head_dim), lambda i, *_: (0, i, 0))
    attended = pl.pallas_call(
        functools.partial(far_kernel, scale),
        grid_spec=pltpu.PrefetchScalarGridSpec(
            num_scalar_prefetch=1,
            grid=(block_len // step,),
            in_specs=[
                some,
                pl.BlockSpec((ctx_size, heads * 2 * ROWS, head_dim), lambda i, *_: (0, 0, 0)),
                some,
                pl.BlockSpec((heads, step), lambda i, *_: (0, i)),
            ],
            out_specs=pl.BlockSpec((step, heads, head_dim), lambda i, *_: (i, 0, 0)),
        ),
        out_shape=jax.ShapeDtypeStruct((block_len, heads, head_dim), BF16),
        compiler_params=params,
        cost_estimate=cost(4, 20),
        name="far",
    )(usable, q, fetched, acc, lse[:, 0])
    return attended, affinity


def solution(mesh):
    in_specs = (
        P("ctx", "head", None),
        P("ctx", "head", None),
        P("ctx", "head", None),
        P(None, "head", None),
    )
    out_specs = (P("ctx", "head", None), P("ctx", "head", None))
    return jax.shard_map(body, mesh=mesh, in_specs=in_specs, out_specs=out_specs, check_vma=False)
```
